32 devices in a mesh: layer: 8 (over y, x, core), dp: 4 (over z).
Axes of the slice: x: 2, y: 2, z: 4, core: 2. Of those that a mesh axis runs over, the one named last changes fastest.
Arguments:
- states_guess: float32 [8, 4, 32, 32, 128], P('layer', 'dp'), may hold values from -6 to 6
- kernels: bfloat16 [8, 9, 128, 128], P('layer'), may hold values from -0.1875 to 0.1875
- adjoint_end: float32 [8, 4, 32, 32, 128], P('layer', 'dp'), may hold values from -6 to 6
- coarse_gain: float32 [8, 128], replicated, may hold values from 0 to 1
Outputs:
- new_states: float32 [8, 4, 32, 32, 128], P('layer', 'dp')
- adjoint_start: float32 [8, 4, 32, 32, 128], P('layer', 'dp')
- weight_grad: float32 [8, 9, 128, 128], P('layer')
- relax_change: float32 [8, 4, 32, 32, 128], P('layer', 'dp')
- adjoint_change: float32 [8, 4, 32, 32, 128], P('layer', 'dp')
The draws below stay inside these ranges and needn't reach their ends.
All inputs are finite; a program needn't handle non-finite values.
Results may differ from the reference program's by a relative error of at most 0.0048.
Values sent between devices are 32-bit elements; how exact they have to be, the bound alone decides.
A program may use at most 64 MiB of HBM per device.

```python
import jax
import jax.numpy as jnp
from jax import lax

CHANNEL_COUNT = 128
SIDE = 32
L_DEV = 1
LAYER_BLOCKS = 8
LAYERS = 8
BATCH = 4


def draw_coarse_gain(key, part):
    random_keys = jax.random.split(key, 5)
    slow_share = 0.5
    slow = jax.random.uniform(random_keys[0], (CHANNEL_COUNT,), jnp.float32) < slow_share
    slow_rate = jax.random.uniform(random_keys[1], (LAYER_BLOCKS, CHANNEL_COUNT), jnp.float32, 0.0, 1.0) / LAYER_BLOCKS
    slow_gain = jnp.exp(-slow_rate)
    fast_gain = jax.random.uniform(random_keys[2], (LAYER_BLOCKS, CHANNEL_COUNT), jnp.float32, 0.1, 0.6)
    blended_states = jnp.where(slow[None, :], slow_gain, fast_gain)
    sweep_rows = jax.random.randint(random_keys[3], (2,), 0, LAYER_BLOCKS)
    rows_per_block = jnp.arange(LAYER_BLOCKS)
    flagged_layers = jnp.any(rows_per_block[:, None] == sweep_rows[None, :], axis=1)
    relax_sweep = jax.random.uniform(random_keys[4], (LAYER_BLOCKS, CHANNEL_COUNT), jnp.float32, 0.6, 0.85)
    blended_states = jnp.where(flagged_layers[:, None], blended_states * relax_sweep, blended_states)
    return blended_states.astype(jnp.float32)


def levels(key, dims, cuts, low, high):
    def one(axis_at, blocks):
        steps = jax.random.uniform(jax.random.fold_in(jax.random.fold_in(key, 6), axis_at), (blocks,), jnp.float32, low / len(cuts), high / len(cuts))
        return jnp.repeat(jnp.exp(steps), dims[axis_at] // blocks).reshape((-1,) + (1,) * (len(dims) - axis_at - 1))

    loudness = one(*cuts[0])
    for cut in cuts[1:]:
        loudness = loudness * one(*cut)
    return loudness


def bell_draw(stream_key, extent, deviation, most, pieces=(), kind=jnp.bfloat16):
    array = deviation * jax.random.normal(stream_key, extent, jnp.float32)
    if pieces:
        array = array * levels(stream_key, extent, pieces, -0.22, 0.18)
    return jnp.clip(array, -most, most).astype(kind)


def setup_inputs(seed: int = 0) -> dict:
    seeds = jax.random.split(jax.random.key(seed), 5)
    return {
        "states_guess": bell_draw(seeds[0], (LAYER_BLOCKS, BATCH, SIDE, SIDE, CHANNEL_COUNT), 1.0, 6.0, ((0, 8), (1, 4)), jnp.float32),
        "kernels": bell_draw(seeds[1], (LAYERS, 9, CHANNEL_COUNT, CHANNEL_COUNT), (9 * CHANNEL_COUNT) ** -0.5, 0.1875, ((0, 8),)),
        "adjoint_end": bell_draw(seeds[2], (LAYER_BLOCKS, BATCH, SIDE, SIDE, CHANNEL_COUNT), 1.0, 6.0, ((0, 8), (1, 4)), jnp.float32),
        "coarse_gain": draw_coarse_gain(jax.random.fold_in(seeds[4], 71), 0),
    }


EPSILON = 1e-06

def stacked_windows(source, flipped):
    images, height, across, channels = source.shape
    padded = jnp.pad(source, ((0, 0), (1, 1), (1, 1), (0, 0)))
    windows = []
    for stencil in range(9):
        if flipped:
            row_start = 2 - stencil // 3
            col_start = 2 - stencil % 3
        else:
            row_start = stencil // 3
            col_start = stencil % 3
        windows.append(padded[:, row_start:row_start + height, col_start:col_start + across, :])
    return jnp.concatenate(windows, axis=3).reshape(images * height * across, 9 * channels)

def conv_apply(source, kernel_set):
    images, height, across, channels = source.shape
    columns = stacked_windows(source, False)
    summed = jnp.dot(columns, kernel_set.reshape(9 * channels, channels), preferred_element_type=jnp.float32)
    return summed.reshape(images, height, across, channels)

def conv_back(source, kernel_set):
    images, height, across, channels = source.shape
    columns = stacked_windows(source, True)
    turned = jnp.transpose(kernel_set, (0, 2, 1)).reshape(9 * channels, channels)
    summed = jnp.dot(columns, turned, preferred_element_type=jnp.float32)
    return summed.reshape(images, height, across, channels)

def conv_weight(source, weighted):
    images, height, across, channels = source.shape
    columns = stacked_windows(source, False)
    flat_error = weighted.reshape(-1, channels)
    result = lax.dot_general(columns, flat_error, (((0,), (0,)), ((), ())), preferred_element_type=jnp.float32)
    return result.reshape(9, channels, channels)

def step_length(layer_pos, layers):
    return (1.0 + 2.0 * layer_pos / (layers - 1)) / layers

def forward_block(start_state, kernel_set, first_layer, layers):
    current = start_state
    for local_pos in range(kernel_set.shape[0]):
        step_len = step_length((first_layer + local_pos).astype(jnp.float32), layers)
        current = current + step_len * jnp.tanh(conv_apply(current.astype(jnp.bfloat16), kernel_set[local_pos]))
    return current

def record_block(start_state, kernel_set, first_layer, layers):
    current = start_state
    stored = []
    slopes = []
    for local_pos in range(kernel_set.shape[0]):
        step_len = step_length((first_layer + local_pos).astype(jnp.float32), layers)
        rounded = current.astype(jnp.bfloat16)
        activation = jnp.tanh(conv_apply(rounded, kernel_set[local_pos]))
        stored.append(rounded)
        slopes.append(1.0 - activation * activation)
        current = current + step_len * activation
    return (jnp.stack(stored), jnp.stack(slopes))

def backward_block(end_state, stored, slopes, kernel_set, first_layer, layers, with_gradient):
    adjoint = end_state
    gradients = []
    for local_pos in reversed(range(kernel_set.shape[0])):
        step_len = step_length((first_layer + local_pos).astype(jnp.float32), layers)
        weighted = (adjoint * slopes[local_pos]).astype(jnp.bfloat16)
        if with_gradient:
            gradients.insert(0, step_len * conv_weight(stored[local_pos], weighted))
        adjoint = adjoint + step_len * conv_back(weighted, kernel_set[local_pos])
    if with_gradient:
        return (adjoint, jnp.stack(gradients))
    return adjoint

def reference(states_guess, kernels, adjoint_end, coarse_gain):
    kernel_blocks = kernels.reshape(LAYER_BLOCKS, L_DEV, 9, CHANNEL_COUNT, CHANNEL_COUNT)
    block_ids = jnp.arange(LAYER_BLOCKS, dtype=jnp.int32)

    def run_forward(starts):
        return lax.map(lambda entries: forward_block(entries[0], entries[1], entries[2] * L_DEV, LAYERS), (starts, kernel_blocks, block_ids))
    anchor = states_guess[0:1]
    first_ends = run_forward(states_guess)
    first_starts = jnp.concatenate([anchor, first_ends[:-1]], axis=0)
    second_ends = run_forward(first_starts)
    second_starts = jnp.concatenate([anchor, second_ends[:-1]], axis=0)
    third_ends = run_forward(second_starts)
    relax_change = third_ends - second_ends
    offsets = third_ends - coarse_gain[:, None, None, None, :] * second_starts

    def coarse_step(running, entries):
        return (entries[0] * running + entries[1], running)
    _, new_states = lax.scan(coarse_step, states_guess[0], (coarse_gain, offsets))
    stored, slopes = lax.map(lambda entries: record_block(entries[0], entries[1], entries[2] * L_DEV, LAYERS), (new_states, kernel_blocks, block_ids))

    def run_backward(ends):
        return lax.map(lambda entries: backward_block(entries[0], entries[1], entries[2], entries[3], entries[4] * L_DEV, LAYERS, False), (ends, stored, slopes, kernel_blocks, block_ids))
    last_end = adjoint_end[-1:]
    first_back = run_backward(adjoint_end)
    adjoint_mid = jnp.concatenate([first_back[1:], last_end], axis=0)
    second_back = run_backward(adjoint_mid)
    adjoint_last = jnp.concatenate([second_back[1:], last_end], axis=0)
    adjoint_start, gradient = lax.map(lambda entries: backward_block(entries[0], entries[1], entries[2], entries[3], entries[4] * L_DEV, LAYERS, True), (adjoint_last, stored, slopes, kernel_blocks, block_ids))
    adjoint_change = adjoint_start - second_back
    gradient = gradient.reshape(LAYERS, 9, CHANNEL_COUNT, CHANNEL_COUNT)
    root_mean = jnp.sqrt(jnp.mean(gradient * gradient) + EPSILON)
    return (new_states, adjoint_start, gradient / root_mean, relax_change, adjoint_change)
```

```python
import functools

import jax
import jax.numpy as jnp
from jax import lax
from jax.experimental import pallas as pl
from jax.experimental.pallas import tpu as pltpu
from jax.sharding import PartitionSpec as P

EPSILON = 1e-06
CHUNKS = 4
LAG = 2


def kernel(
    L, Z, side, anchor, kern, aend, gain,
    ns, ast, gsum, sqsum, rc, ac,
    tx, rx, off, xcf, xcd, slopes, xt, wb, gacc, gout_rx, gin_rx, sqrx, sqtx,
    send_sem, recv_sem, gsend_in, grecv_out, gsend_out, grecv_in, sq_send, sq_recv,
):
    n, ch = anchor.shape
    nc = CHUNKS
    R = n // nc
    pos = lax.axis_index("layer")
    zp = lax.axis_index("dp")
    is_first, is_last = pos == 0, pos == L - 1
    not_first, not_last = pos > 0, pos < L - 1
    half = Z // 2
    on_left = zp < half
    inward = jnp.where(on_left, zp + 1, zp - 1)
    has_out = (zp > 0) & (zp < Z - 1)
    no_out = (zp == 0) | (zp == Z - 1)
    outward = jnp.where(no_out, zp, jnp.where(on_left, zp - 1, zp + 1))
    is_mid = (zp == half - 1) | (zp == half)
    not_mid = (zp < half - 1) | (zp > half)
    h = (1.0 + 2.0 * pos.astype(jnp.float32) / (L - 1)) / L

    barrier = pltpu.get_barrier_semaphore()
    for k in range(1, L):
        pl.semaphore_signal(
            barrier, inc=1, device_id={"layer": lax.rem(pos + k, L)},
            device_id_type=pl.DeviceIdType.MESH,
        )
    pl.semaphore_signal(barrier, inc=1, device_id={"dp": inward}, device_id_type=pl.DeviceIdType.MESH)

    @pl.when(has_out)
    def _():
        pl.semaphore_signal(barrier, inc=1, device_id={"dp": outward}, device_id_type=pl.DeviceIdType.MESH)

    def rows(c):
        return pl.ds(c * R, R)

    def link(phase, c, dst):
        return pltpu.make_async_remote_copy(
            src_ref=tx.at[phase, rows(c)],
            dst_ref=rx.at[phase, rows(c)],
            send_sem=send_sem.at[phase, c],
            recv_sem=recv_sem.at[phase, c],
            device_id={"layer": dst},
            device_id_type=pl.DeviceIdType.MESH,
        )

    up = lax.rem(pos + 1, L)
    down = lax.rem(pos + L - 1, L)

    def send(phase, c):
        if phase < 3:
            pl.when(not_last)(lambda: link(phase, c, up).start())
        else:
            pl.when(not_first)(lambda: link(phase, c, down).start())

    def arrive(phase, c):
        if phase < 3:
            pl.when(not_first)(lambda: link(phase, c, up).wait_recv())
        else:
            pl.when(not_last)(lambda: link(phase, c, down).wait_recv())

    def sent(phase, c):
        if phase < 3:
            pl.when(not_last)(lambda: link(phase, c, up).wait_send())
        else:
            pl.when(not_first)(lambda: link(phase, c, down).wait_send())

    across = lax.broadcasted_iota(jnp.int32, (R, ch), 0) % side
    left_ok = across > 0
    right_ok = across < side - 1

    def stage(xc, c, value):
        at = pl.ds(side + c * R, R)
        xc[at, 0:ch] = jnp.where(left_ok, pltpu.roll(value, 1, 0), 0.0).astype(jnp.bfloat16)
        xc[at, ch : 2 * ch] = value.astype(jnp.bfloat16)
        xc[at, 2 * ch : 3 * ch] = jnp.where(right_ok, pltpu.roll(value, R - 1, 0), 0.0).astype(jnp.bfloat16)

    def conv(xc, w, c):
        total = None
        for d in range(3):
            term = jnp.dot(
                xc[pl.ds(c * R + side * d, R), :], w[d], preferred_element_type=jnp.float32
            )
            total = term if total is None else total + term
        return total

    zeros = jnp.zeros((side, 3 * ch), jnp.bfloat16)
    for xc in (xcf, xcd):
        xc[0:side, :] = zeros
        xc[n + side : n + 2 * side, :] = zeros

    for c in range(nc):
        stage(xcf, c, anchor[rows(c), :])
    for c in range(nc):
        tx[0, rows(c), :] = anchor[rows(c), :] + h * jnp.tanh(conv(xcf, kern, c))
        if c == 0:
            pl.semaphore_wait(barrier, jnp.where(has_out, L + 1, L))
        send(0, c)

    @pl.when(is_first)
    def _():
        for p in range(3):
            rx[p] = anchor[...]

    @pl.when(is_last)
    def _():
        for p in range(3, 5):
            rx[p] = aend[...]

    for d in range(3):
        for e in range(3):
            tap = kern[2 - d, (2 - e) * ch : (3 - e) * ch, :]
            wb[d, e * ch : (e + 1) * ch, :] = tap.astype(jnp.float32).T.astype(jnp.bfloat16)

    block_gain = gain[pl.ds(pos, 1), :]

    def second(c):
        tx[1, rows(c), :] = rx[0, rows(c), :] + h * jnp.tanh(conv(xcf, kern, c))
        send(1, c)

    for c in range(nc):
        arrive(0, c)
        stage(xcf, c, rx[0, rows(c), :])
        if c > 0:
            second(c - 1)
    second(nc - 1)

    def third(c):
        start = rx[1, rows(c), :]
        end = start + h * jnp.tanh(conv(xcf, kern, c))
        rc[rows(c), :] = end - tx[1, rows(c), :]
        off[rows(c), :] = end - block_gain * start

    for c in range(nc):
        arrive(1, c)
        stage(xcf, c, rx[1, rows(c), :])
        if c > 0:
            third(c - 1)
    third(nc - 1)

    def record(c):
        act = jnp.tanh(conv(xcf, kern, c))
        slopes[rows(c), :] = 1.0 - act * act
        xt[:, rows(c)] = xcf[pl.ds(side + c * R, R), :].T

    for c in range(nc):
        arrive(2, c)
        state = rx[2, rows(c), :]
        tx[2, rows(c), :] = block_gain * state + off[rows(c), :]
        send(2, c)
        ns[rows(c), :] = state
        stage(xcf, c, state)
        if c > 0:
            record(c - 1)
    record(nc - 1)

    for c in range(nc):
        stage(xcd, c, aend[rows(c), :] * slopes[rows(c), :])
    for c in range(nc):
        tx[3, rows(c), :] = aend[rows(c), :] + h * conv(xcd, wb, c)
        send(3, c)

    def second_back(c):
        tx[4, rows(c), :] = rx[3, rows(c), :] + h * conv(xcd, wb, c)
        send(4, c)

    for c in range(nc):
        arrive(3, c)
        stage(xcd, c, rx[3, rows(c), :] * slopes[rows(c), :])
        if c > 0:
            second_back(c - 1)
    second_back(nc - 1)

    for c in range(nc):
        arrive(4, c)
        stage(xcd, c, rx[4, rows(c), :] * slopes[rows(c), :])

    def g_in(t, dst):
        return pltpu.make_async_remote_copy(
            src_ref=gacc.at[t], dst_ref=dst.at[t], send_sem=gsend_in.at[t],
            recv_sem=(grecv_out if dst is gout_rx else grecv_in).at[t],
            device_id={"dp": inward}, device_id_type=pl.DeviceIdType.MESH,
        )

    def g_out(t):
        return pltpu.make_async_remote_copy(
            src_ref=gsum.at[t], dst_ref=gin_rx.at[t], send_sem=gsend_out.at[t],
            recv_sem=grecv_in.at[t], device_id={"dp": outward},
            device_id_type=pl.DeviceIdType.MESH,
        )

    def push(t):
        pl.when(is_mid)(lambda: g_in(t, gin_rx).start())
        pl.when(not_mid)(lambda: g_in(t, gout_rx).start())

    for d in range(3):
        three = h * jnp.dot(
            xt[...], xcd[pl.ds((2 - d) * side, n), ch : 2 * ch], preferred_element_type=jnp.float32
        )
        for e in range(3):
            gacc[3 * d + e] = three[e * ch : (e + 1) * ch, :]

            @pl.when(no_out)
            def _(t=3 * d + e):
                push(t)

    def towards(t):
        @pl.when(has_out)
        def _():
            g_in(t, gout_rx).wait_recv()
            gacc[t] = gacc[t] + gout_rx[t]
            push(t)

    def outwards(t):
        g_in(t, gin_rx).wait_recv()

        @pl.when(is_mid)
        def _():
            gsum[t] = gacc[t] + gin_rx[t]

        @pl.when(not_mid)
        def _():
            gsum[t] = gin_rx[t]

        pl.when(has_out)(lambda: g_out(t).start())

    def finish(c):
        done = rx[4, rows(c), :] + h * conv(xcd, wb, c)
        ast[rows(c), :] = done
        ac[rows(c), :] = done - tx[4, rows(c), :]

    squares = jnp.zeros((8, ch), jnp.float32)
    for t in range(9 + LAG):
        if t < 9:
            towards(t)
        if t < nc:
            finish(t)
        if t >= LAG:
            outwards(t - LAG)
            block = gsum[t - LAG]
            squares = squares + jnp.sum((block * block).reshape(ch // 8, 8, ch), axis=0)

    sqtx[...] = squares

    def sq(k):
        return pltpu.make_async_remote_copy(
            src_ref=sqtx, dst_ref=sqrx.at[k - 1], send_sem=sq_send.at[k - 1],
            recv_sem=sq_recv.at[k - 1], device_id={"layer": lax.rem(pos + k, L)},
            device_id_type=pl.DeviceIdType.MESH,
        )

    for k in range(1, L):
        sq(k).start()
    for p in range(5):
        for c in range(nc):
            sent(p, c)
    for t in range(9):
        g_in(t, gin_rx).wait_send()
        pl.when(has_out)(lambda t=t: g_out(t).wait_send())
    for k in range(1, L):
        sq(k).wait_recv()
        squares = squares + sqrx[k - 1]
    sqsum[...] = squares
    for k in range(1, L):
        sq(k).wait_send()


def local(L, Z, states_guess, kernels, adjoint_end, coarse_gain):
    side, ch = states_guess.shape[2], states_guess.shape[4]
    images = states_guess.shape[1]
    n = images * side * side
    f32, bf16 = jnp.float32, jnp.bfloat16
    state = jax.ShapeDtypeStruct((n, ch), f32)
    vm = pl.BlockSpec(memory_space=pltpu.VMEM)
    V = pltpu.VMEM
    D = pltpu.SemaphoreType.DMA
    ns, ast, gsum, sq, rc, ac = pl.pallas_call(
        functools.partial(kernel, L, Z, side),
        out_shape=(
            state, state, jax.ShapeDtypeStruct((9, ch, ch), f32),
            jax.ShapeDtypeStruct((8, ch), f32), state, state,
        ),
        in_specs=[vm] * 4,
        out_specs=(vm,) * 6,
        scratch_shapes=[
            V((5, n, ch), f32), V((5, n, ch), f32), V((n, ch), f32),
            V((n + 2 * side, 3 * ch), bf16), V((n + 2 * side, 3 * ch), bf16),
            V((n, ch), f32), V((3 * ch, n), bf16), V((3, 3 * ch, ch), bf16),
            V((9, ch, ch), f32), V((9, ch, ch), f32), V((9, ch, ch), f32),
            V((L - 1, 8, ch), f32), V((8, ch), f32),
            D((5, CHUNKS)), D((5, CHUNKS)), D((9,)), D((9,)), D((9,)), D((9,)),
            D((L - 1,)), D((L - 1,)),
        ],
        compiler_params=pltpu.CompilerParams(
            collective_id=0, has_side_effects=True, vmem_limit_bytes=48 * 1024 * 1024
        ),
    )(
        states_guess.reshape(n, ch), kernels.reshape(3, 3 * ch, ch),
        adjoint_end.reshape(n, ch), coarse_gain,
    )
    weight_grad = gsum / jnp.sqrt(jnp.sum(sq) / (L * 9 * ch * ch) + EPSILON)
    full = states_guess.shape
    return (
        ns.reshape(full), ast.reshape(full), weight_grad.reshape(1, 9, ch, ch),
        rc.reshape(full), ac.reshape(full),
    )


def solution(mesh):
    in_specs = (
        P("layer", "dp", None, None, None),
        P("layer", None, None, None),
        P("layer", "dp", None, None, None),
        P(),
    )
    out_specs = (
        P("layer", "dp", None, None, None),
        P("layer", "dp", None, None, None),
        P("layer", None, None, None),
        P("layer", "dp", None, None, None),
        P("layer", "dp", None, None, None),
    )
    fn = functools.partial(local, mesh.shape["layer"], mesh.shape["dp"])
    return jax.shard_map(fn, mesh=mesh, in_specs=in_specs, out_specs=out_specs, check_vma=False)
```

```python
import functools

import jax
import jax.numpy as jnp
from jax import lax
from jax.experimental import pallas as pl
from jax.experimental.pallas import tpu as pltpu
from jax.sharding import PartitionSpec as P

EPSILON = 1e-06
CHUNKS = 4
LAG = 2


def kernel(
    L, Z, side, anchor_hbm, kern_hbm, aend_hbm, gain,
    ns_hbm, ast_hbm, gsum_hbm, sqsum, rc_hbm, ac_hbm,
    ns, ast, gsum, rc, ac, anchor, kern, aend, tx, rx, off, off_rx,  xcf, xcd, slopes, xt, wb, gacc, gout_rx, gin_rx, sqrx, sqtx,
    in_sem, out_sem, gout_sem, send_sem, recv_sem, off_send, off_recv, relay_sem, gsend_in, grecv_out, gsend_out, grecv_in, sq_send, sq_recv,
):
    loads = [
        pltpu.make_async_copy(a, b, in_sem.at[i])
        for i, (a, b) in enumerate(((anchor_hbm, anchor), (kern_hbm, kern), (aend_hbm, aend)))
    ]
    for load in loads:
        load.start()
    stores = [
        pltpu.make_async_copy(a, b, out_sem.at[i])
        for i, (a, b) in enumerate(((ns, ns_hbm), (ast, ast_hbm), (rc, rc_hbm), (ac, ac_hbm)))
    ]

    def gstore(t):
        return pltpu.make_async_copy(gsum.at[t], gsum_hbm.at[t], gout_sem.at[t])

    n, ch = anchor.shape
    nc = CHUNKS
    R = n // nc
    pos = lax.axis_index("layer")
    zp = lax.axis_index("dp")
    is_first, is_last = pos == 0, pos == L - 1
    not_first, not_last = pos > 0, pos < L - 1
    half = Z // 2
    on_left = zp < half
    inward = jnp.where(on_left, zp + 1, zp - 1)
    has_out = (zp > 0) & (zp < Z - 1)
    no_out = (zp == 0) | (zp == Z - 1)
    outward = jnp.where(no_out, zp, jnp.where(on_left, zp - 1, zp + 1))
    is_mid = (zp == half - 1) | (zp == half)
    not_mid = (zp < half - 1) | (zp > half)
    h = (1.0 + 2.0 * pos.astype(jnp.float32) / (L - 1)) / L

    barrier = pltpu.get_barrier_semaphore()
    for k in range(1, L):
        pl.semaphore_signal(
            barrier, inc=1, device_id={"layer": lax.rem(pos + k, L)},
            device_id_type=pl.DeviceIdType.MESH,
        )
    pl.semaphore_signal(barrier, inc=1, device_id={"dp": inward}, device_id_type=pl.DeviceIdType.MESH)

    @pl.when(has_out)
    def _():
        pl.semaphore_signal(barrier, inc=1, device_id={"dp": outward}, device_id_type=pl.DeviceIdType.MESH)

    def rows(c):
        return pl.ds(c * R, R)

    def link(phase, c, dst):
        return pltpu.make_async_remote_copy(
            src_ref=tx.at[phase, rows(c)],
            dst_ref=rx.at[phase, rows(c)],
            send_sem=send_sem.at[phase, c],
            recv_sem=recv_sem.at[phase, c],
            device_id={"layer": dst},
            device_id_type=pl.DeviceIdType.MESH,
        )

    up = lax.rem(pos + 1, L)
    down = lax.rem(pos + L - 1, L)
    odd = lax.rem(pos, 2) == 1
    ahead = jnp.where(odd, lax.rem(pos + 2, L), up)
    paired_even = (pos >= 4) & (lax.rem(pos, 2) == 0)
    paired_odd = (pos >= 5) & odd
    target = (up, up, ahead, down, down)
    sends = (
        not_last,
        (pos > 0) & (pos < L - 1),
        (pos == 2) | ((pos >= 3) & (pos < L - 2) & odd),
        not_first,
        (pos > 0) & (pos < L - 1),
    )
    gets = (not_first, pos > 1, pos > 2, not_last, pos < L - 2)

    def send(phase, c):
        pl.when(sends[phase])(lambda: link(phase, c, target[phase]).start())

    def arrive(phase, c):
        pl.when(gets[phase])(lambda: link(phase, c, target[phase]).wait_recv())

    def sent(phase, c):
        pl.when(sends[phase])(lambda: link(phase, c, target[phase]).wait_send())

    def off_link(c):
        return pltpu.make_async_remote_copy(
            src_ref=off.at[rows(c)], dst_ref=off_rx.at[rows(c)], send_sem=off_send.at[c],
            recv_sem=off_recv.at[c], device_id={"layer": up},
            device_id_type=pl.DeviceIdType.MESH,
        )

    def relay(c):
        return pltpu.make_async_remote_copy(
            src_ref=rx.at[2, rows(c)], dst_ref=rx.at[2, rows(c)], send_sem=relay_sem.at[c],
            recv_sem=recv_sem.at[2, c], device_id={"layer": down},
            device_id_type=pl.DeviceIdType.MESH,
        )

    across = lax.broadcasted_iota(jnp.int32, (R, ch), 0) % side
    left_ok = across > 0
    right_ok = across < side - 1

    def stage(xc, c, value):
        at = pl.ds(side + c * R, R)
        xc[at, 0:ch] = jnp.where(left_ok, pltpu.roll(value, 1, 0), 0.0).astype(jnp.bfloat16)
        xc[at, ch : 2 * ch] = value.astype(jnp.bfloat16)
        xc[at, 2 * ch : 3 * ch] = jnp.where(right_ok, pltpu.roll(value, R - 1, 0), 0.0).astype(jnp.bfloat16)

    def conv(xc, w, c):
        total = None
        for d in range(3):
            term = jnp.dot(
                xc[pl.ds(c * R + side * d, R), :], w[d], preferred_element_type=jnp.float32
            )
            total = term if total is None else total + term
        return total

    zeros = jnp.zeros((side, 3 * ch), jnp.bfloat16)
    for xc in (xcf, xcd):
        xc[0:side, :] = zeros
        xc[n + side : n + 2 * side, :] = zeros

    loads[0].wait()
    loads[1].wait()
    for c in range(nc):
        stage(xcf, c, anchor[rows(c), :])
    for c in range(nc):
        tx[0, rows(c), :] = anchor[rows(c), :] + h * jnp.tanh(conv(xcf, kern, c))
        if c == 0:
            pl.semaphore_wait(barrier, jnp.where(has_out, L + 1, L))
        send(0, c)

    @pl.when(is_first)
    def _():
        for p in range(2):
            rx[p] = anchor[...]

    loads[2].wait()

    @pl.when(is_last)
    def _():
        for p in range(3, 5):
            rx[p] = aend[...]

    for d in range(3):
        for e in range(3):
            tap = kern[2 - d, (2 - e) * ch : (3 - e) * ch, :]
            wb[d, e * ch : (e + 1) * ch, :] = tap.astype(jnp.float32).T.astype(jnp.bfloat16)

    block_gain = gain[pl.ds(pos, 1), :]
    before_gain = gain[pl.ds(jnp.maximum(pos - 1, 0), 1), :]

    def second(c):
        tx[1, rows(c), :] = rx[0, rows(c), :] + h * jnp.tanh(conv(xcf, kern, c))
        send(1, c)

    for c in range(nc):
        arrive(0, c)
        stage(xcf, c, rx[0, rows(c), :])

        @pl.when(pos == 1)
        def _():
            rx[1, rows(c), :] = rx[0, rows(c), :]

        if c > 0:
            second(c - 1)
    second(nc - 1)

    def third(c):
        start = rx[1, rows(c), :]
        end = start + h * jnp.tanh(conv(xcf, kern, c))
        rc[rows(c), :] = end - tx[1, rows(c), :]
        off[rows(c), :] = end - block_gain * start
        pl.when(paired_even)(lambda: off_link(c).start())

    for c in range(nc):
        arrive(1, c)
        stage(xcf, c, rx[1, rows(c), :])
        if c > 0:
            third(c - 1)
    third(nc - 1)
    stores[2].start()

    def record(c):
        act = jnp.tanh(conv(xcf, kern, c))
        slopes[rows(c), :] = 1.0 - act * act
        xt[:, rows(c)] = xcf[pl.ds(side + c * R, R), :].T

    for c in range(nc):
        arrive(2, c)

        @pl.when(pos <= 2)
        def _():
            ns[rows(c), :] = rx[1, rows(c), :]

        @pl.when((pos == 3) | paired_even)
        def _():
            ns[rows(c), :] = rx[2, rows(c), :]

        @pl.when(paired_odd)
        def _():
            relay(c).start()
            off_link(c).wait_recv()
            ns[rows(c), :] = before_gain * rx[2, rows(c), :] + off_rx[rows(c), :]

        state = ns[rows(c), :]
        tx[2, rows(c), :] = block_gain * state + off[rows(c), :]
        send(2, c)
        stage(xcf, c, state)
        if c > 0:
            record(c - 1)
    record(nc - 1)
    stores[0].start()

    for c in range(nc):
        stage(xcd, c, aend[rows(c), :] * slopes[rows(c), :])
    for c in range(nc):
        tx[3, rows(c), :] = aend[rows(c), :] + h * conv(xcd, wb, c)
        send(3, c)

    def second_back(c):
        tx[4, rows(c), :] = rx[3, rows(c), :] + h * conv(xcd, wb, c)
        send(4, c)

    for c in range(nc):
        arrive(3, c)
        stage(xcd, c, rx[3, rows(c), :] * slopes[rows(c), :])

        @pl.when(pos == L - 2)
        def _():
            rx[4, rows(c), :] = rx[3, rows(c), :]

        if c > 0:
            second_back(c - 1)
    second_back(nc - 1)

    for c in range(nc):
        arrive(4, c)
        stage(xcd, c, rx[4, rows(c), :] * slopes[rows(c), :])

    def g_in(t, dst):
        return pltpu.make_async_remote_copy(
            src_ref=gacc.at[t], dst_ref=dst.at[t], send_sem=gsend_in.at[t],
            recv_sem=(grecv_out if dst is gout_rx else grecv_in).at[t],
            device_id={"dp": inward}, device_id_type=pl.DeviceIdType.MESH,
        )

    def g_out(t):
        return pltpu.make_async_remote_copy(
            src_ref=gsum.at[t], dst_ref=gin_rx.at[t], send_sem=gsend_out.at[t],
            recv_sem=grecv_in.at[t], device_id={"dp": outward},
            device_id_type=pl.DeviceIdType.MESH,
        )

    def push(t):
        pl.when(is_mid)(lambda: g_in(t, gin_rx).start())
        pl.when(not_mid)(lambda: g_in(t, gout_rx).start())

    for d in range(3):
        three = h * jnp.dot(
            xt[...], xcd[pl.ds((2 - d) * side, n), ch : 2 * ch], preferred_element_type=jnp.float32
        )
        for e in range(3):
            gacc[3 * d + e] = three[e * ch : (e + 1) * ch, :]

            @pl.when(no_out)
            def _(t=3 * d + e):
                push(t)

    def towards(t):
        @pl.when(has_out)
        def _():
            g_in(t, gout_rx).wait_recv()
            gacc[t] = gacc[t] + gout_rx[t]
            push(t)

    def outwards(t):
        g_in(t, gin_rx).wait_recv()

        @pl.when(is_mid)
        def _():
            gsum[t] = gacc[t] + gin_rx[t]

        @pl.when(not_mid)
        def _():
            gsum[t] = gin_rx[t]

        pl.when(has_out)(lambda: g_out(t).start())
        gstore(t).start()

    def finish(c):
        done = rx[4, rows(c), :] + h * conv(xcd, wb, c)
        ast[rows(c), :] = done
        ac[rows(c), :] = done - tx[4, rows(c), :]

    squares = jnp.zeros((8, ch), jnp.float32)
    for t in range(9 + LAG):
        if t < 9:
            towards(t)
        if t < nc:
            finish(t)
        if t == nc:
            stores[1].start()
            stores[3].start()
        if t >= LAG:
            outwards(t - LAG)
            block = gsum[t - LAG]
            squares = squares + jnp.sum((block * block).reshape(ch // 8, 8, ch), axis=0)

    sqtx[...] = squares

    def sq(k):
        return pltpu.make_async_remote_copy(
            src_ref=sqtx, dst_ref=sqrx.at[k - 1], send_sem=sq_send.at[k - 1],
            recv_sem=sq_recv.at[k - 1], device_id={"layer": lax.rem(pos + k, L)},
            device_id_type=pl.DeviceIdType.MESH,
        )

    for k in range(1, L):
        sq(k).start()
    for p in range(5):
        for c in range(nc):
            sent(p, c)
    for c in range(nc):
        pl.when(paired_even)(lambda c=c: off_link(c).wait_send())
        pl.when(paired_odd)(lambda c=c: relay(c).wait_send())
    for t in range(9):
        g_in(t, gin_rx).wait_send()
        gstore(t).wait()
        pl.when(has_out)(lambda t=t: g_out(t).wait_send())
    for store in stores:
        store.wait()
    for k in range(1, L):
        sq(k).wait_recv()
        squares = squares + sqrx[k - 1]
    sqsum[...] = squares
    for k in range(1, L):
        sq(k).wait_send()


def write_out(
    entries, ns, ast, gsum, sq, rc, ac, ns_hbm, ast_hbm, wg_hbm, rc_hbm, ac_hbm, g, wg, sem, gsem, wsem
):
    load = pltpu.make_async_copy(gsum, g, gsem)
    load.start()
    pairs = ((ns, ns_hbm), (ast, ast_hbm), (rc, rc_hbm), (ac, ac_hbm))
    copies = [pltpu.make_async_copy(a, b, sem.at[i]) for i, (a, b) in enumerate(pairs)]
    for copy in copies:
        copy.start()
    mean = jnp.sum(sq[...], keepdims=True) / entries
    root = jnp.sqrt(mean + EPSILON)
    load.wait()
    for d in range(3):
        at = pl.ds(3 * d, 3)
        wg[at] = g[at] / root[None]
        copy = pltpu.make_async_copy(wg.at[at], wg_hbm.at[at], wsem.at[d])
        copy.start()
        copies.append(copy)
    for copy in copies:
        copy.wait()


def local(L, Z, states_guess, kernels, adjoint_end, coarse_gain):
    side, ch = states_guess.shape[2], states_guess.shape[4]
    images = states_guess.shape[1]
    n = images * side * side
    f32, bf16 = jnp.float32, jnp.bfloat16
    state = jax.ShapeDtypeStruct((n, ch), f32)
    vm = pl.BlockSpec(memory_space=pltpu.VMEM)
    hbm = pl.BlockSpec(memory_space=pltpu.HBM)
    V = pltpu.VMEM
    D = pltpu.SemaphoreType.DMA
    ns, ast, gsum, sq, rc, ac = pl.pallas_call(
        functools.partial(kernel, L, Z, side),
        out_shape=(
            state, state, jax.ShapeDtypeStruct((9, ch, ch), f32),
            jax.ShapeDtypeStruct((8, ch), f32), state, state,
        ),
        in_specs=[hbm] * 3 + [vm],
        out_specs=(hbm, hbm, hbm, vm, hbm, hbm),
        scratch_shapes=[
            V((n, ch), f32), V((n, ch), f32), V((9, ch, ch), f32), V((n, ch), f32), V((n, ch), f32),
            V((n, ch), f32), V((3, 3 * ch, ch), bf16), V((n, ch), f32),
            V((5, n, ch), f32), V((5, n, ch), f32), V((n, ch), f32), V((n, ch), f32),
            V((n + 2 * side, 3 * ch), bf16), V((n + 2 * side, 3 * ch), bf16),
            V((n, ch), f32), V((3 * ch, n), bf16), V((3, 3 * ch, ch), bf16),
            V((9, ch, ch), f32), V((9, ch, ch), f32), V((9, ch, ch), f32),
            V((L - 1, 8, ch), f32), V((8, ch), f32),
            D((3,)), D((4,)), D((9,)), D((5, CHUNKS)), D((5, CHUNKS)), D((CHUNKS,)), D((CHUNKS,)), D((CHUNKS,)), D((9,)), D((9,)), D((9,)), D((9,)),
            D((L - 1,)), D((L - 1,)),
        ],
        compiler_params=pltpu.CompilerParams(
            collective_id=0, has_side_effects=True, vmem_limit_bytes=62 * 1024 * 1024
        ),
    )(
        states_guess.reshape(n, ch), kernels.reshape(3, 3 * ch, ch),
        adjoint_end.reshape(n, ch), coarse_gain,
    )
    ns, ast, weight_grad, rc, ac = pl.pallas_call(
        functools.partial(write_out, L * 9 * ch * ch),
        out_shape=(state, state, jax.ShapeDtypeStruct((9, ch, ch), f32), state, state),
        in_specs=[hbm, hbm, hbm, vm, hbm, hbm],
        out_specs=(hbm,) * 5,
        scratch_shapes=[V((9, ch, ch), f32), V((9, ch, ch), f32), D((4,)), D, D((3,))],
        compiler_params=pltpu.CompilerParams(vmem_limit_bytes=62 * 1024 * 1024),
    )(ns, ast, gsum, sq, rc, ac)
    full = states_guess.shape
    return (
        ns.reshape(full), ast.reshape(full), weight_grad.reshape(1, 9, ch, ch),
        rc.reshape(full), ac.reshape(full),
    )


def solution(mesh):
    in_specs = (
        P("layer", "dp", None, None, None),
        P("layer", None, None, None),
        P("layer", "dp", None, None, None),
        P(),
    )
    out_specs = (
        P("layer", "dp", None, None, None),
        P("layer", "dp", None, None, None),
        P("layer", None, None, None),
        P("layer", "dp", None, None, None),
        P("layer", "dp", None, None, None),
    )
    fn = functools.partial(local, mesh.shape["layer"], mesh.shape["dp"])
    return jax.shard_map(fn, mesh=mesh, in_specs=in_specs, out_specs=out_specs, check_vma=False)
```

```python
import functools

import jax
import jax.numpy as jnp
from jax import lax
from jax.experimental import pallas as pl
from jax.experimental.pallas import tpu as pltpu
from jax.sharding import PartitionSpec as P

EPSILON = 1e-06
CHUNKS = 8
LAG = 3
PIECES = 18


def kernel(
    L, Z, side, anchor_hbm, kern_hbm, aend_hbm, gain,
    ns_hbm, ast_hbm, gsum_hbm, sqsum, rc_hbm, ac_hbm,
    ns, ast, gsum, rc, ac, anchor, kern, aend, tx, rx, off, off_rx,  xcf, xcd, slopes, xt, wb, gacc, gout_rx, gin_rx, sqrx, sqtx,
    in_sem, out_sem, gout_sem, send_sem, recv_sem, off_send, off_recv, relay_sem, gsend_in, grecv_out, gsend_out, grecv_in, sq_send, sq_recv,
):
    loads = [
        pltpu.make_async_copy(a, b, in_sem.at[i])
        for i, (a, b) in enumerate(((anchor_hbm, anchor), (kern_hbm, kern), (aend_hbm, aend)))
    ]
    for load in loads:
        load.start()
    stores = [
        pltpu.make_async_copy(a, b, out_sem.at[i])
        for i, (a, b) in enumerate(((ns, ns_hbm), (ast, ast_hbm), (rc, rc_hbm), (ac, ac_hbm)))
    ]

    def gstore(t):
        return pltpu.make_async_copy(gsum.at[t], gsum_hbm.at[t], gout_sem.at[t])

    n, ch = anchor.shape
    nc = CHUNKS
    R = n // nc
    pos = lax.axis_index("layer")
    zp = lax.axis_index("dp")
    is_first, is_last = pos == 0, pos == L - 1
    not_first, not_last = pos > 0, pos < L - 1
    half = Z // 2
    on_left = zp < half
    inward = jnp.where(on_left, zp + 1, zp - 1)
    has_out = (zp > 0) & (zp < Z - 1)
    no_out = (zp == 0) | (zp == Z - 1)
    outward = jnp.where(no_out, zp, jnp.where(on_left, zp - 1, zp + 1))
    is_mid = (zp == half - 1) | (zp == half)
    not_mid = (zp < half - 1) | (zp > half)
    h = (1.0 + 2.0 * pos.astype(jnp.float32) / (L - 1)) / L

    barrier = pltpu.get_barrier_semaphore()
    for k in range(1, L):
        pl.semaphore_signal(
            barrier, inc=1, device_id={"layer": lax.rem(pos + k, L)},
            device_id_type=pl.DeviceIdType.MESH,
        )
    pl.semaphore_signal(barrier, inc=1, device_id={"dp": inward}, device_id_type=pl.DeviceIdType.MESH)

    @pl.when(has_out)
    def _():
        pl.semaphore_signal(barrier, inc=1, device_id={"dp": outward}, device_id_type=pl.DeviceIdType.MESH)

    def rows(c):
        return pl.ds(c * R, R)

    def link(phase, c, dst):
        return pltpu.make_async_remote_copy(
            src_ref=tx.at[phase, rows(c)],
            dst_ref=rx.at[phase, rows(c)],
            send_sem=send_sem.at[phase, c],
            recv_sem=recv_sem.at[phase, c],
            device_id={"layer": dst},
            device_id_type=pl.DeviceIdType.MESH,
        )

    up = lax.rem(pos + 1, L)
    down = lax.rem(pos + L - 1, L)
    odd = lax.rem(pos, 2) == 1
    ahead = jnp.where(odd, lax.rem(pos + 2, L), up)
    paired_even = (pos >= 4) & (lax.rem(pos, 2) == 0)
    paired_odd = (pos >= 5) & odd
    target = (up, up, ahead, down, down)
    sends = (
        not_last,
        (pos > 0) & (pos < L - 1),
        (pos == 2) | ((pos >= 3) & (pos < L - 2) & odd),
        not_first,
        (pos > 0) & (pos < L - 1),
    )
    gets = (not_first, pos > 1, pos > 2, not_last, pos < L - 2)

    def send(phase, c):
        pl.when(sends[phase])(lambda: link(phase, c, target[phase]).start())

    def arrive(phase, c):
        pl.when(gets[phase])(lambda: link(phase, c, target[phase]).wait_recv())

    def sent(phase, c):
        pl.when(sends[phase])(lambda: link(phase, c, target[phase]).wait_send())

    def off_link(c):
        return pltpu.make_async_remote_copy(
            src_ref=off.at[rows(c)], dst_ref=off_rx.at[rows(c)], send_sem=off_send.at[c],
            recv_sem=off_recv.at[c], device_id={"layer": up},
            device_id_type=pl.DeviceIdType.MESH,
        )

    def relay(c):
        return pltpu.make_async_remote_copy(
            src_ref=rx.at[2, rows(c)], dst_ref=rx.at[2, rows(c)], send_sem=relay_sem.at[c],
            recv_sem=recv_sem.at[2, c], device_id={"layer": down},
            device_id_type=pl.DeviceIdType.MESH,
        )

    across = lax.broadcasted_iota(jnp.int32, (R, ch), 0) % side
    left_ok = across > 0
    right_ok = across < side - 1

    def stage(xc, c, value):
        at = pl.ds(side + c * R, R)
        xc[at, 0:ch] = jnp.where(left_ok, pltpu.roll(value, 1, 0), 0.0).astype(jnp.bfloat16)
        xc[at, ch : 2 * ch] = value.astype(jnp.bfloat16)
        xc[at, 2 * ch : 3 * ch] = jnp.where(right_ok, pltpu.roll(value, R - 1, 0), 0.0).astype(jnp.bfloat16)

    def conv(xc, w, c):
        total = None
        for d in range(3):
            term = jnp.dot(
                xc[pl.ds(c * R + side * d, R), :], w[d], preferred_element_type=jnp.float32
            )
            total = term if total is None else total + term
        return total

    zeros = jnp.zeros((side, 3 * ch), jnp.bfloat16)
    for xc in (xcf, xcd):
        xc[0:side, :] = zeros
        xc[n + side : n + 2 * side, :] = zeros

    loads[0].wait()
    loads[1].wait()
    for c in range(nc):
        stage(xcf, c, anchor[rows(c), :])
    for c in range(nc):
        tx[0, rows(c), :] = anchor[rows(c), :] + h * jnp.tanh(conv(xcf, kern, c))
        if c == 0:
            pl.semaphore_wait(barrier, jnp.where(has_out, L + 1, L))
        send(0, c)

    @pl.when(is_first)
    def _():
        for p in range(2):
            rx[p] = anchor[...]

    loads[2].wait()

    @pl.when(is_last)
    def _():
        for p in range(3, 5):
            rx[p] = aend[...]

    for d in range(3):
        for e in range(3):
            tap = kern[2 - d, (2 - e) * ch : (3 - e) * ch, :]
            wb[d, e * ch : (e + 1) * ch, :] = tap.astype(jnp.float32).T.astype(jnp.bfloat16)

    block_gain = gain[pl.ds(pos, 1), :]
    before_gain = gain[pl.ds(jnp.maximum(pos - 1, 0), 1), :]

    def second(c):
        tx[1, rows(c), :] = rx[0, rows(c), :] + h * jnp.tanh(conv(xcf, kern, c))
        send(1, c)

    for c in range(nc):
        arrive(0, c)
        stage(xcf, c, rx[0, rows(c), :])

        @pl.when(pos == 1)
        def _():
            rx[1, rows(c), :] = rx[0, rows(c), :]

        if c > 0:
            second(c - 1)
    second(nc - 1)

    def third(c):
        start = rx[1, rows(c), :]
        end = start + h * jnp.tanh(conv(xcf, kern, c))
        rc[rows(c), :] = end - tx[1, rows(c), :]
        off[rows(c), :] = end - block_gain * start
        pl.when(paired_even)(lambda: off_link(c).start())

    for c in range(nc):
        arrive(1, c)
        stage(xcf, c, rx[1, rows(c), :])
        if c > 0:
            third(c - 1)
    third(nc - 1)
    stores[2].start()

    def record(c):
        act = jnp.tanh(conv(xcf, kern, c))
        slopes[rows(c), :] = 1.0 - act * act
        xt[:, rows(c)] = xcf[pl.ds(side + c * R, R), :].T

    for c in range(nc):
        arrive(2, c)

        @pl.when(pos <= 2)
        def _():
            ns[rows(c), :] = rx[1, rows(c), :]

        @pl.when((pos == 3) | paired_even)
        def _():
            ns[rows(c), :] = rx[2, rows(c), :]

        @pl.when(paired_odd)
        def _():
            relay(c).start()
            off_link(c).wait_recv()
            ns[rows(c), :] = before_gain * rx[2, rows(c), :] + off_rx[rows(c), :]

        state = ns[rows(c), :]
        tx[2, rows(c), :] = block_gain * state + off[rows(c), :]
        send(2, c)
        stage(xcf, c, state)
        if c > 0:
            record(c - 1)
    record(nc - 1)
    stores[0].start()

    for c in range(nc):
        stage(xcd, c, aend[rows(c), :] * slopes[rows(c), :])
    for c in range(nc):
        tx[3, rows(c), :] = aend[rows(c), :] + h * conv(xcd, wb, c)
        send(3, c)

    def second_back(c):
        tx[4, rows(c), :] = rx[3, rows(c), :] + h * conv(xcd, wb, c)
        send(4, c)

    for c in range(nc):
        arrive(3, c)
        stage(xcd, c, rx[3, rows(c), :] * slopes[rows(c), :])

        @pl.when(pos == L - 2)
        def _():
            rx[4, rows(c), :] = rx[3, rows(c), :]

        if c > 0:
            second_back(c - 1)
    second_back(nc - 1)

    for c in range(nc):
        arrive(4, c)
        stage(xcd, c, rx[4, rows(c), :] * slopes[rows(c), :])

    def g_in(t, dst):
        return pltpu.make_async_remote_copy(
            src_ref=gacc.at[t], dst_ref=dst.at[t], send_sem=gsend_in.at[t],
            recv_sem=(grecv_out if dst is gout_rx else grecv_in).at[t],
            device_id={"dp": inward}, device_id_type=pl.DeviceIdType.MESH,
        )

    def g_out(t):
        return pltpu.make_async_remote_copy(
            src_ref=gsum.at[t], dst_ref=gin_rx.at[t], send_sem=gsend_out.at[t],
            recv_sem=grecv_in.at[t], device_id={"dp": outward},
            device_id_type=pl.DeviceIdType.MESH,
        )

    def push(t):
        pl.when(is_mid)(lambda: g_in(t, gin_rx).start())
        pl.when(not_mid)(lambda: g_in(t, gout_rx).start())

    for d in range(3):
        three = h * jnp.dot(
            xt[...], xcd[pl.ds((2 - d) * side, n), ch : 2 * ch], preferred_element_type=jnp.float32
        )
        each = PIECES // 3
        deep = 3 * ch // each
        for e in range(each):
            gacc[each * d + e] = three[e * deep : (e + 1) * deep, :]

            @pl.when(no_out)
            def _(t=each * d + e):
                push(t)

    def towards(t):
        @pl.when(has_out)
        def _():
            g_in(t, gout_rx).wait_recv()
            gacc[t] = gacc[t] + gout_rx[t]
            push(t)

    def outwards(t):
        g_in(t, gin_rx).wait_recv()

        @pl.when(is_mid)
        def _():
            gsum[t] = gacc[t] + gin_rx[t]

        @pl.when(not_mid)
        def _():
            gsum[t] = gin_rx[t]

        pl.when(has_out)(lambda: g_out(t).start())
        gstore(t).start()

    def finish(c):
        done = rx[4, rows(c), :] + h * conv(xcd, wb, c)
        ast[rows(c), :] = done
        ac[rows(c), :] = done - tx[4, rows(c), :]

    squares = jnp.zeros((8, ch), jnp.float32)
    for t in range(PIECES + LAG):
        if t < PIECES:
            towards(t)
        if t < nc:
            finish(t)
        if t == nc:
            stores[1].start()
            stores[3].start()
        if t >= LAG:
            outwards(t - LAG)
            block = gsum[t - LAG]
            squares = squares + jnp.sum((block * block).reshape(-1, 8, ch), axis=0)

    sqtx[...] = squares

    def sq(k):
        return pltpu.make_async_remote_copy(
            src_ref=sqtx, dst_ref=sqrx.at[k - 1], send_sem=sq_send.at[k - 1],
            recv_sem=sq_recv.at[k - 1], device_id={"layer": lax.rem(pos + k, L)},
            device_id_type=pl.DeviceIdType.MESH,
        )

    for k in range(1, L):
        sq(k).start()
    for p in range(5):
        for c in range(nc):
            sent(p, c)
    for c in range(nc):
        pl.when(paired_even)(lambda c=c: off_link(c).wait_send())
        pl.when(paired_odd)(lambda c=c: relay(c).wait_send())
    for t in range(PIECES):
        g_in(t, gin_rx).wait_send()
        gstore(t).wait()
        pl.when(has_out)(lambda t=t: g_out(t).wait_send())
    for store in stores:
        store.wait()
    for k in range(1, L):
        sq(k).wait_recv()
        squares = squares + sqrx[k - 1]
    sqsum[...] = squares
    for k in range(1, L):
        sq(k).wait_send()


def write_out(
    entries, ns, ast, gsum, sq, rc, ac, ns_hbm, ast_hbm, wg_hbm, rc_hbm, ac_hbm,
    held, g, wg, in_sem, sem, gsem, wsem,
):
    pairs = ((ns, ns_hbm), (ast, ast_hbm), (rc, rc_hbm), (ac, ac_hbm))
    loads = [pltpu.make_async_copy(a, held.at[i], in_sem.at[i]) for i, (a, b) in enumerate(pairs)]
    copies = [pltpu.make_async_copy(held.at[i], b, sem.at[i]) for i, (a, b) in enumerate(pairs)]
    first = pltpu.make_async_copy(gsum, g, gsem)
    first.start()
    for load in loads:
        load.start()
    mean = jnp.sum(sq[...], keepdims=True) / entries
    root = jnp.sqrt(mean + EPSILON)
    first.wait()
    for d in range(3):
        at = pl.ds(3 * d, 3)
        wg[at] = g[at] / root[None]
        copy = pltpu.make_async_copy(wg.at[at], wg_hbm.at[at], wsem.at[d])
        copy.start()
        copies.append(copy)
    for load, copy in zip(loads, copies[:4]):
        load.wait()
        copy.start()
    for copy in copies:
        copy.wait()


def local(L, Z, states_guess, kernels, adjoint_end, coarse_gain):
    side, ch = states_guess.shape[2], states_guess.shape[4]
    images = states_guess.shape[1]
    n = images * side * side
    f32, bf16 = jnp.float32, jnp.bfloat16
    state = jax.ShapeDtypeStruct((n, ch), f32)
    parts = (PIECES, 9 * ch // PIECES, ch)
    vm = pl.BlockSpec(memory_space=pltpu.VMEM)
    hbm = pl.BlockSpec(memory_space=pltpu.HBM)
    V = pltpu.VMEM
    D = pltpu.SemaphoreType.DMA
    ns, ast, gsum, sq, rc, ac = pl.pallas_call(
        functools.partial(kernel, L, Z, side),
        out_shape=(
            state, state, jax.ShapeDtypeStruct(parts, f32),
            jax.ShapeDtypeStruct((8, ch), f32), state, state,
        ),
        in_specs=[hbm] * 3 + [vm],
        out_specs=(hbm, hbm, hbm, vm, hbm, hbm),
        scratch_shapes=[
            V((n, ch), f32), V((n, ch), f32), V(parts, f32), V((n, ch), f32), V((n, ch), f32),
            V((n, ch), f32), V((3, 3 * ch, ch), bf16), V((n, ch), f32),
            V((5, n, ch), f32), V((5, n, ch), f32), V((n, ch), f32), V((n, ch), f32),
            V((n + 2 * side, 3 * ch), bf16), V((n + 2 * side, 3 * ch), bf16),
            V((n, ch), f32), V((3 * ch, n), bf16), V((3, 3 * ch, ch), bf16),
            V(parts, f32), V(parts, f32), V(parts, f32),
            V((L - 1, 8, ch), f32), V((8, ch), f32),
            D((3,)), D((4,)), D((PIECES,)), D((5, CHUNKS)), D((5, CHUNKS)), D((CHUNKS,)), D((CHUNKS,)), D((CHUNKS,)), D((PIECES,)), D((PIECES,)), D((PIECES,)), D((PIECES,)),
            D((L - 1,)), D((L - 1,)),
        ],
        compiler_params=pltpu.CompilerParams(
            collective_id=0, has_side_effects=True, vmem_limit_bytes=62 * 1024 * 1024
        ),
    )(
        states_guess.reshape(n, ch), kernels.reshape(3, 3 * ch, ch),
        adjoint_end.reshape(n, ch), coarse_gain,
    )
    ns, ast, weight_grad, rc, ac = pl.pallas_call(
        functools.partial(write_out, L * 9 * ch * ch),
        out_shape=(state, state, jax.ShapeDtypeStruct((9, ch, ch), f32), state, state),
        in_specs=[hbm, hbm, hbm, vm, hbm, hbm],
        out_specs=(hbm,) * 5,
        scratch_shapes=[
            V((4, n, ch), f32), V((9, ch, ch), f32), V((9, ch, ch), f32),
            D((4,)), D((4,)), D, D((3,)),
        ],
        compiler_params=pltpu.CompilerParams(vmem_limit_bytes=62 * 1024 * 1024),
    )(ns, ast, gsum.reshape(9, ch, ch), sq, rc, ac)
    full = states_guess.shape
    return (
        ns.reshape(full), ast.reshape(full), weight_grad.reshape(1, 9, ch, ch),
        rc.reshape(full), ac.reshape(full),
    )


def solution(mesh):
    in_specs = (
        P("layer", "dp", None, None, None),
        P("layer", None, None, None),
        P("layer", "dp", None, None, None),
        P(),
    )
    out_specs = (
        P("layer", "dp", None, None, None),
        P("layer", "dp", None, None, None),
        P("layer", None, None, None),
        P("layer", "dp", None, None, None),
        P("layer", "dp", None, None, None),
    )
    fn = functools.partial(local, mesh.shape["layer"], mesh.shape["dp"])
    return jax.shard_map(fn, mesh=mesh, in_specs=in_specs, out_specs=out_specs, check_vma=False)
```

```python
import functools

import jax
import jax.numpy as jnp
from jax import lax
from jax.experimental import pallas as pl
from jax.experimental.pallas import tpu as pltpu
from jax.sharding import PartitionSpec as P

EPSILON = 1e-06
CHUNKS = 8
LAG = 3
PIECES = 18


def kernel(
    L, Z, side, anchor_hbm, kern_hbm, aend_hbm, gain,
    ns_hbm, ast_hbm, gsum_hbm, sqsum, rc_hbm, ac_hbm,
    ns, ast, gsum, rc, ac, anchor, kern, aend, tx, rx, off, off_rx,  xcf, xcd, slopes, xt, wb, gacc, gout_rx, gin_rx, sqrx, sqtx,
    in_sem, out_sem, gout_sem, send_sem, recv_sem, off_send, off_recv, relay_sem, gsend_in, grecv_out, gsend_out, grecv_in, sq_send, sq_recv,
):
    loads = [
        pltpu.make_async_copy(a, b, in_sem.at[i])
        for i, (a, b) in enumerate(((anchor_hbm, anchor), (kern_hbm, kern), (aend_hbm, aend)))
    ]
    for load in loads:
        load.start()
    stores = [
        pltpu.make_async_copy(a, b, out_sem.at[i])
        for i, (a, b) in enumerate(((ns, ns_hbm), (ast, ast_hbm), (rc, rc_hbm), (ac, ac_hbm)))
    ]

    def gstore(t):
        return pltpu.make_async_copy(gsum.at[t], gsum_hbm.at[t], gout_sem.at[t])

    n, ch = anchor.shape
    nc = CHUNKS
    R = n // nc
    pos = lax.axis_index("layer")
    zp = lax.axis_index("dp")
    is_first, is_last = pos == 0, pos == L - 1
    not_first, not_last = pos > 0, pos < L - 1
    half = Z // 2
    on_left = zp < half
    inward = jnp.where(on_left, zp + 1, zp - 1)
    has_out = (zp > 0) & (zp < Z - 1)
    no_out = (zp == 0) | (zp == Z - 1)
    outward = jnp.where(no_out, zp, jnp.where(on_left, zp - 1, zp + 1))
    is_mid = (zp == half - 1) | (zp == half)
    not_mid = (zp < half - 1) | (zp > half)
    h = (1.0 + 2.0 * pos.astype(jnp.float32) / (L - 1)) / L

    barrier = pltpu.get_barrier_semaphore()
    for k in range(1, L):
        pl.semaphore_signal(
            barrier, inc=1, device_id={"layer": lax.rem(pos + k, L)},
            device_id_type=pl.DeviceIdType.MESH,
        )
    pl.semaphore_signal(barrier, inc=1, device_id={"dp": inward}, device_id_type=pl.DeviceIdType.MESH)

    @pl.when(has_out)
    def _():
        pl.semaphore_signal(barrier, inc=1, device_id={"dp": outward}, device_id_type=pl.DeviceIdType.MESH)

    def rows(c):
        return pl.ds(c * R, R)

    def link(phase, c, dst):
        return pltpu.make_async_remote_copy(
            src_ref=tx.at[phase, rows(c)],
            dst_ref=rx.at[phase, rows(c)],
            send_sem=send_sem.at[phase, c],
            recv_sem=recv_sem.at[phase, c],
            device_id={"layer": dst},
            device_id_type=pl.DeviceIdType.MESH,
        )

    up = lax.rem(pos + 1, L)
    down = lax.rem(pos + L - 1, L)
    odd = lax.rem(pos, 2) == 1
    ahead = jnp.where(odd, lax.rem(pos + 2, L), up)
    paired_even = (pos >= 4) & (lax.rem(pos, 2) == 0)
    paired_odd = (pos >= 5) & odd
    target = (up, up, ahead, down, down)
    sends = (
        not_last,
        (pos > 0) & (pos < L - 1),
        (pos == 2) | ((pos >= 3) & (pos < L - 2) & odd),
        not_first,
        (pos > 0) & (pos < L - 1),
    )
    gets = (not_first, pos > 1, pos > 2, not_last, pos < L - 2)

    def send(phase, c):
        pl.when(sends[phase])(lambda: link(phase, c, target[phase]).start())

    def arrive(phase, c):
        pl.when(gets[phase])(lambda: link(phase, c, target[phase]).wait_recv())

    def sent(phase, c):
        pl.when(sends[phase])(lambda: link(phase, c, target[phase]).wait_send())

    def off_link(c):
        return pltpu.make_async_remote_copy(
            src_ref=off.at[rows(c)], dst_ref=off_rx.at[rows(c)], send_sem=off_send.at[c],
            recv_sem=off_recv.at[c], device_id={"layer": up},
            device_id_type=pl.DeviceIdType.MESH,
        )

    def relay(c):
        return pltpu.make_async_remote_copy(
            src_ref=rx.at[2, rows(c)], dst_ref=rx.at[2, rows(c)], send_sem=relay_sem.at[c],
            recv_sem=recv_sem.at[2, c], device_id={"layer": down},
            device_id_type=pl.DeviceIdType.MESH,
        )

    across = lax.broadcasted_iota(jnp.int32, (R, ch), 0) % side
    left_ok = across > 0
    right_ok = across < side - 1

    def stage(xc, c, value):
        at = pl.ds(side + c * R, R)
        xc[at, 0:ch] = jnp.where(left_ok, pltpu.roll(value, 1, 0), 0.0).astype(jnp.bfloat16)
        xc[at, ch : 2 * ch] = value.astype(jnp.bfloat16)
        xc[at, 2 * ch : 3 * ch] = jnp.where(right_ok, pltpu.roll(value, R - 1, 0), 0.0).astype(jnp.bfloat16)

    def conv(xc, w, c):
        total = None
        for d in range(3):
            term = jnp.dot(
                xc[pl.ds(c * R + side * d, R), :], w[d], preferred_element_type=jnp.float32
            )
            total = term if total is None else total + term
        return total

    zeros = jnp.zeros((side, 3 * ch), jnp.bfloat16)
    for xc in (xcf, xcd):
        xc[0:side, :] = zeros
        xc[n + side : n + 2 * side, :] = zeros

    loads[0].wait()
    loads[1].wait()
    for c in range(nc):
        stage(xcf, c, anchor[rows(c), :])
    for c in range(nc):
        tx[0, rows(c), :] = anchor[rows(c), :] + h * jnp.tanh(conv(xcf, kern, c))
        if c == 0:
            pl.semaphore_wait(barrier, jnp.where(has_out, L + 1, L))
        send(0, c)

    @pl.when(is_first)
    def _():
        for p in range(2):
            rx[p] = anchor[...]

    loads[2].wait()

    @pl.when(is_last)
    def _():
        for p in range(3, 5):
            rx[p] = aend[...]

    for d in range(3):
        for e in range(3):
            tap = kern[2 - d, (2 - e) * ch : (3 - e) * ch, :]
            wb[d, e * ch : (e + 1) * ch, :] = tap.astype(jnp.float32).T.astype(jnp.bfloat16)

    block_gain = gain[pl.ds(pos, 1), :]
    before_gain = gain[pl.ds(jnp.maximum(pos - 1, 0), 1), :]

    def second(c):
        tx[1, rows(c), :] = rx[0, rows(c), :] + h * jnp.tanh(conv(xcf, kern, c))
        send(1, c)

    for c in range(nc):
        arrive(0, c)
        stage(xcf, c, rx[0, rows(c), :])

        @pl.when(pos == 1)
        def _():
            rx[1, rows(c), :] = rx[0, rows(c), :]

        if c > 0:
            second(c - 1)
    second(nc - 1)

    def third(c):
        start = rx[1, rows(c), :]
        end = start + h * jnp.tanh(conv(xcf, kern, c))
        rc[rows(c), :] = end - tx[1, rows(c), :]
        off[rows(c), :] = end - block_gain * start
        pl.when(paired_even)(lambda: off_link(c).start())

    for c in range(nc):
        arrive(1, c)
        stage(xcf, c, rx[1, rows(c), :])
        if c > 0:
            third(c - 1)
    third(nc - 1)
    stores[2].start()

    def record(c):
        act = jnp.tanh(conv(xcf, kern, c))
        slopes[rows(c), :] = 1.0 - act * act

    for c in range(nc):
        arrive(2, c)

        @pl.when(pos <= 2)
        def _():
            ns[rows(c), :] = rx[1, rows(c), :]

        @pl.when((pos == 3) | paired_even)
        def _():
            ns[rows(c), :] = rx[2, rows(c), :]

        @pl.when(paired_odd)
        def _():
            relay(c).start()
            off_link(c).wait_recv()
            ns[rows(c), :] = before_gain * rx[2, rows(c), :] + off_rx[rows(c), :]

        state = ns[rows(c), :]
        tx[2, rows(c), :] = block_gain * state + off[rows(c), :]
        send(2, c)
        stage(xcf, c, state)
        if c > 0:
            record(c - 1)
    record(nc - 1)
    stores[0].start()

    for c in range(nc):
        stage(xcd, c, aend[rows(c), :] * slopes[rows(c), :])
    for c in range(nc):
        tx[3, rows(c), :] = aend[rows(c), :] + h * conv(xcd, wb, c)
        send(3, c)
    for c in range(nc):
        xt[:, rows(c)] = xcf[pl.ds(side + c * R, R), :].T

    def second_back(c):
        tx[4, rows(c), :] = rx[3, rows(c), :] + h * conv(xcd, wb, c)
        send(4, c)

    for c in range(nc):
        arrive(3, c)
        stage(xcd, c, rx[3, rows(c), :] * slopes[rows(c), :])

        @pl.when(pos == L - 2)
        def _():
            rx[4, rows(c), :] = rx[3, rows(c), :]

        if c > 0:
            second_back(c - 1)
    second_back(nc - 1)

    for c in range(nc):
        arrive(4, c)
        stage(xcd, c, rx[4, rows(c), :] * slopes[rows(c), :])

    def g_in(t, dst):
        return pltpu.make_async_remote_copy(
            src_ref=gacc.at[t], dst_ref=dst.at[t], send_sem=gsend_in.at[t],
            recv_sem=(grecv_out if dst is gout_rx else grecv_in).at[t],
            device_id={"dp": inward}, device_id_type=pl.DeviceIdType.MESH,
        )

    def g_out(t):
        return pltpu.make_async_remote_copy(
            src_ref=gsum.at[t], dst_ref=gin_rx.at[t], send_sem=gsend_out.at[t],
            recv_sem=grecv_in.at[t], device_id={"dp": outward},
            device_id_type=pl.DeviceIdType.MESH,
        )

    def push(t):
        pl.when(is_mid)(lambda: g_in(t, gin_rx).start())
        pl.when(not_mid)(lambda: g_in(t, gout_rx).start())

    for d in range(3):
        three = h * jnp.dot(
            xt[...], xcd[pl.ds((2 - d) * side, n), ch : 2 * ch], preferred_element_type=jnp.float32
        )
        each = PIECES // 3
        deep = 3 * ch // each
        for e in range(each):
            gacc[each * d + e] = three[e * deep : (e + 1) * deep, :]

            @pl.when(no_out)
            def _(t=each * d + e):
                push(t)

    def towards(t):
        @pl.when(has_out)
        def _():
            g_in(t, gout_rx).wait_recv()
            gacc[t] = gacc[t] + gout_rx[t]
            push(t)

    def outwards(t):
        g_in(t, gin_rx).wait_recv()

        @pl.when(is_mid)
        def _():
            gsum[t] = gacc[t] + gin_rx[t]

        @pl.when(not_mid)
        def _():
            gsum[t] = gin_rx[t]

        pl.when(has_out)(lambda: g_out(t).start())
        gstore(t).start()

    def finish(c):
        done = rx[4, rows(c), :] + h * conv(xcd, wb, c)
        ast[rows(c), :] = done
        ac[rows(c), :] = done - tx[4, rows(c), :]

    squares = jnp.zeros((8, ch), jnp.float32)
    for t in range(PIECES + LAG):
        if t < PIECES:
            towards(t)
        if t < nc:
            finish(t)
        if t == nc:
            stores[1].start()
            stores[3].start()
        if t >= LAG:
            outwards(t - LAG)
            block = gsum[t - LAG]
            squares = squares + jnp.sum((block * block).reshape(-1, 8, ch), axis=0)

    sqtx[...] = squares

    def sq(k):
        return pltpu.make_async_remote_copy(
            src_ref=sqtx, dst_ref=sqrx.at[k - 1], send_sem=sq_send.at[k - 1],
            recv_sem=sq_recv.at[k - 1], device_id={"layer": lax.rem(pos + k, L)},
            device_id_type=pl.DeviceIdType.MESH,
        )

    for k in range(1, L):
        sq(k).start()
    for p in range(5):
        for c in range(nc):
            sent(p, c)
    for c in range(nc):
        pl.when(paired_even)(lambda c=c: off_link(c).wait_send())
        pl.when(paired_odd)(lambda c=c: relay(c).wait_send())
    for t in range(PIECES):
        g_in(t, gin_rx).wait_send()
        gstore(t).wait()
        pl.when(has_out)(lambda t=t: g_out(t).wait_send())
    for store in stores:
        store.wait()
    for k in range(1, L):
        sq(k).wait_recv()
        squares = squares + sqrx[k - 1]
    sqsum[...] = squares
    for k in range(1, L):
        sq(k).wait_send()


def write_out(
    entries, ns, ast, gsum, sq, rc, ac, ns_hbm, ast_hbm, wg_hbm, rc_hbm, ac_hbm,
    held, g, wg, in_sem, sem, gsem, wsem,
):
    pairs = ((ns, ns_hbm), (ast, ast_hbm), (rc, rc_hbm), (ac, ac_hbm))
    loads = [pltpu.make_async_copy(a, held.at[i], in_sem.at[i]) for i, (a, b) in enumerate(pairs)]
    copies = [pltpu.make_async_copy(held.at[i], b, sem.at[i]) for i, (a, b) in enumerate(pairs)]
    first = pltpu.make_async_copy(gsum, g, gsem)
    first.start()
    for load in loads:
        load.start()
    mean = jnp.sum(sq[...], keepdims=True) / entries
    root = jnp.sqrt(mean + EPSILON)
    first.wait()
    for d in range(3):
        at = pl.ds(3 * d, 3)
        wg[at] = g[at] / root[None]
        copy = pltpu.make_async_copy(wg.at[at], wg_hbm.at[at], wsem.at[d])
        copy.start()
        copies.append(copy)
    for load, copy in zip(loads, copies[:4]):
        load.wait()
        copy.start()
    for copy in copies:
        copy.wait()


def local(L, Z, states_guess, kernels, adjoint_end, coarse_gain):
    side, ch = states_guess.shape[2], states_guess.shape[4]
    images = states_guess.shape[1]
    n = images * side * side
    f32, bf16 = jnp.float32, jnp.bfloat16
    state = jax.ShapeDtypeStruct((n, ch), f32)
    parts = (PIECES, 9 * ch // PIECES, ch)
    vm = pl.BlockSpec(memory_space=pltpu.VMEM)
    hbm = pl.BlockSpec(memory_space=pltpu.HBM)
    V = pltpu.VMEM
    D = pltpu.SemaphoreType.DMA
    ns, ast, gsum, sq, rc, ac = pl.pallas_call(
        functools.partial(kernel, L, Z, side),
        out_shape=(
            state, state, jax.ShapeDtypeStruct(parts, f32),
            jax.ShapeDtypeStruct((8, ch), f32), state, state,
        ),
        in_specs=[hbm] * 3 + [vm],
        out_specs=(hbm, hbm, hbm, vm, hbm, hbm),
        scratch_shapes=[
            V((n, ch), f32), V((n, ch), f32), V(parts, f32), V((n, ch), f32), V((n, ch), f32),
            V((n, ch), f32), V((3, 3 * ch, ch), bf16), V((n, ch), f32),
            V((5, n, ch), f32), V((5, n, ch), f32), V((n, ch), f32), V((n, ch), f32),
            V((n + 2 * side, 3 * ch), bf16), V((n + 2 * side, 3 * ch), bf16),
            V((n, ch), f32), V((3 * ch, n), bf16), V((3, 3 * ch, ch), bf16),
            V(parts, f32), V(parts, f32), V(parts, f32),
            V((L - 1, 8, ch), f32), V((8, ch), f32),
            D((3,)), D((4,)), D((PIECES,)), D((5, CHUNKS)), D((5, CHUNKS)), D((CHUNKS,)), D((CHUNKS,)), D((CHUNKS,)), D((PIECES,)), D((PIECES,)), D((PIECES,)), D((PIECES,)),
            D((L - 1,)), D((L - 1,)),
        ],
        compiler_params=pltpu.CompilerParams(
            collective_id=0, has_side_effects=True, vmem_limit_bytes=62 * 1024 * 1024
        ),
    )(
        states_guess.reshape(n, ch), kernels.reshape(3, 3 * ch, ch),
        adjoint_end.reshape(n, ch), coarse_gain,
    )
    ns, ast, weight_grad, rc, ac = pl.pallas_call(
        functools.partial(write_out, L * 9 * ch * ch),
        out_shape=(state, state, jax.ShapeDtypeStruct((9, ch, ch), f32), state, state),
        in_specs=[hbm, hbm, hbm, vm, hbm, hbm],
        out_specs=(hbm,) * 5,
        scratch_shapes=[
            V((4, n, ch), f32), V((9, ch, ch), f32), V((9, ch, ch), f32),
            D((4,)), D((4,)), D, D((3,)),
        ],
        compiler_params=pltpu.CompilerParams(vmem_limit_bytes=62 * 1024 * 1024),
    )(ns, ast, gsum.reshape(9, ch, ch), sq, rc, ac)
    full = states_guess.shape
    return (
        ns.reshape(full), ast.reshape(full), weight_grad.reshape(1, 9, ch, ch),
        rc.reshape(full), ac.reshape(full),
    )


def solution(mesh):
    in_specs = (
        P("layer", "dp", None, None, None),
        P("layer", None, None, None),
        P("layer", "dp", None, None, None),
        P(),
    )
    out_specs = (
        P("layer", "dp", None, None, None),
        P("layer", "dp", None, None, None),
        P("layer", None, None, None),
        P("layer", "dp", None, None, None),
        P("layer", "dp", None, None, None),
    )
    fn = functools.partial(local, mesh.shape["layer"], mesh.shape["dp"])
    return jax.shard_map(fn, mesh=mesh, in_specs=in_specs, out_specs=out_specs, check_vma=False)
```
